128 devices in a mesh: ctx: 8 (over z_hi, x), tp: 16 (over z_lo, y, core).
Axes of the slice: x: 4, y: 4, z: 4 (z_hi: 2, z_lo: 2; z = z_hi * 2 + z_lo), core: 2. Of those that a mesh axis runs over, the one named last changes fastest.
Arguments:
- query_gate: bfloat16 [4096, 8192], P('ctx', 'tp'), may hold values from -6 to 6
- key_gate: bfloat16 [4096, 8192], P('ctx', 'tp'), may hold values from -6 to 6
- value_input: bfloat16 [4096, 8192], P('ctx', 'tp'), may hold values from -6 to 6
- filter_taps: float32 [4096, 512], P('ctx', 'tp'), may hold values from -6 to 6
- out_weight: bfloat16 [8192, 8192], P('tp'), may hold values from -0.09375 to 0.09375
- out_grad: bfloat16 [4096, 8192], P('ctx', 'tp'), may hold values from -6 to 6
Outputs:
- projected: bfloat16 [4096, 8192], P('ctx', 'tp')
- grad_query: bfloat16 [4096, 8192], P('ctx', 'tp')
- grad_key: bfloat16 [4096, 8192], P('ctx', 'tp')
- grad_value: bfloat16 [4096, 8192], P('ctx', 'tp')
- grad_filter: float32 [4096, 512], P('ctx', 'tp')
The draws below stay inside these ranges and needn't reach their ends.
All inputs are finite; a program needn't handle non-finite values.
Results may differ from the reference program's by a relative error of at most 0.027.
Values may be sent and summed in bfloat16 or wider, within the bound.
A program may use at most 192 MiB of HBM per device.

```python
import math
import jax
import jax.numpy as jnp
from jax import lax

D = 8192
GROUP = 16
SEQ = 4096
GROUPS = 512
N_TP = 16


def raised(values, rng, source, target, shards_of, factor):
    owner, partner = [(jnp.arange(values.shape[axis_at]) // (values.shape[axis_at] // shards_of)).reshape([-1 if axis == axis_at else 1 for axis in range(values.ndim)]) for axis_at in (source, target)]
    chosen = jax.random.permutation(rng, shards_of)[partner]
    strong = (owner == chosen) | (owner == (partner + shards_of // 2) % shards_of)
    return jnp.where(strong, factor * values, values)


def steps_of(stream_key, extent, split, low, largest):
    def one(axis_at, shards_of):
        steps = jax.random.uniform(jax.random.fold_in(jax.random.fold_in(stream_key, 6), axis_at), (shards_of,), jnp.float32, low / len(split), largest / len(split))
        return jnp.repeat(jnp.exp(steps), extent[axis_at] // shards_of).reshape((-1,) + (1,) * (len(extent) - axis_at - 1))

    loudness = one(*split[0])
    for cut in split[1:]:
        loudness = loudness * one(*cut)
    return loudness


def bell_draw(rng, dims, width, most, pieces=(), kind=jnp.bfloat16):
    level = steps_of(rng, dims, pieces, -0.22, 0.18) if pieces else 1.0
    result = jax.random.normal(rng, dims, jnp.float32) * width * level
    return jnp.minimum(jnp.maximum(result, -most), most).astype(kind)


def bell_draw_with(key, dims, spread, most, split, heavy, dtype=jnp.bfloat16):
    array = spread * jax.random.normal(key, dims, jnp.float32)
    if split:
        array = array * steps_of(key, dims, split, -0.22, 0.18)
    return jnp.clip(raised(array, jax.random.fold_in(key, 3), *heavy), -most, most).astype(dtype)


def setup_inputs(seed: int = 0) -> dict:
    key_list = jax.random.split(jax.random.key(seed), 7)
    return {
        "query_gate": bell_draw(key_list[0], (SEQ, D), 1.0, 6.0, ((0, 8), (1, 16))),
        "key_gate": bell_draw(key_list[1], (SEQ, D), 1.0, 6.0, ((0, 8), (1, 16))),
        "value_input": bell_draw(key_list[2], (SEQ, D), 1.0, 6.0, ((0, 8), (1, 16))),
        "filter_taps": bell_draw(key_list[3], (SEQ, GROUPS), 1.0, 6.0, ((0, 8), (1, 16)), jnp.float32),
        "out_weight": bell_draw_with(key_list[4], (D, D), D ** -0.5, 0.09375, ((0, 16),), (0, 1, 16, 2.0)),
        "out_grad": bell_draw(key_list[5], (SEQ, D), 1.0, 6.0, ((0, 8), (1, 16))),
    }


def reference(query_gate, key_gate, value_input, filter_taps, out_weight, out_grad):
    seq_len, model_width = query_gate.shape
    tap_scale = 1.0 / math.sqrt(seq_len)
    fft_len = 2 * seq_len
    product_in = (key_gate.astype(jnp.float32) * value_input.astype(jnp.float32)).astype(jnp.bfloat16)
    tap_rows = filter_taps * tap_scale
    tap_spec = jnp.repeat(jnp.fft.rfft(tap_rows, n=fft_len, axis=0), GROUP, axis=1)
    input_spec = jnp.fft.rfft(product_in.astype(jnp.float32), n=fft_len, axis=0)
    convolved = jnp.fft.irfft(input_spec * tap_spec, n=fft_len, axis=0)[:seq_len]
    gated_out = (query_gate.astype(jnp.float32) * convolved).astype(jnp.bfloat16)
    block_width = model_width // N_TP
    projected = jnp.zeros((seq_len, model_width), jnp.float32)
    for block_no in range(N_TP):
        block_begin = block_no * block_width
        block_end = block_begin + block_width
        block_sum = jnp.dot(gated_out[:, block_begin:block_end], out_weight[block_begin:block_end], preferred_element_type=jnp.float32).astype(jnp.bfloat16)
        block_sum = lax.optimization_barrier(block_sum)
        projected = projected + block_sum.astype(jnp.float32)
    projected = projected.astype(jnp.bfloat16)
    dgated = jnp.dot(out_grad, out_weight.T, preferred_element_type=jnp.float32).astype(jnp.bfloat16)
    grad_query = (dgated.astype(jnp.float32) * convolved).astype(jnp.bfloat16)
    conv_grad = (dgated.astype(jnp.float32) * query_gate.astype(jnp.float32)).astype(jnp.bfloat16)
    grad_spec = jnp.fft.rfft(conv_grad.astype(jnp.float32), n=fft_len, axis=0)
    input_grad = jnp.fft.irfft(jnp.conj(tap_spec) * grad_spec, n=fft_len, axis=0)[:seq_len]
    grad_key = (input_grad * value_input.astype(jnp.float32)).astype(jnp.bfloat16)
    grad_value = (input_grad * key_gate.astype(jnp.float32)).astype(jnp.bfloat16)
    cross_spec = (grad_spec * jnp.conj(input_spec)).reshape(grad_spec.shape[0], model_width // GROUP, GROUP).sum(axis=2)
    grad_filter = jnp.fft.irfft(cross_spec, n=fft_len, axis=0)[:seq_len] * tap_scale
    return (projected, grad_query, grad_key, grad_value, grad_filter)
```

```python
import math

import jax
import jax.numpy as jnp
from jax import lax
from jax.experimental import pallas as pl
from jax.experimental.pallas import tpu as pltpu
from jax.sharding import PartitionSpec as P

B=256; H=128
def build_tb(tb_ref, g, taps_row):
    L=taps_row.shape[1]
    z=jnp.zeros((1,H),jnp.float32)
    v=jnp.broadcast_to(jnp.concatenate([z,taps_row,z],axis=1),(16,L+2*H))
    base=pltpu.roll(v,0,1,stride=1,stride_axis=0)
    for k in range(H//16):
        r=pltpu.roll(base,16*k,1) if k else base
        tb_ref[g,16*k:16*k+16,:]=r.astype(jnp.bfloat16)
def tmat(tb_ref,g):
    L=tb_ref.shape[2]-2*H
    return jnp.concatenate([tb_ref[g,:,H:H+L],tb_ref[g,:,0:L]],axis=0)
def conv_fwd(xp_ref, tb_ref, g):
    R=xp_ref.shape[1]//2; nb=R//16
    acc=None
    xs=[xp_ref[g,R-16*d:2*R-16*d,:] for d in range(nb)]
    ts=[jnp.concatenate([tb_ref[g,:,H+B*d:H+B*d+B],tb_ref[g,:,B*d:B*d+B]],axis=0) for d in range(nb)]
    return jnp.dot(jnp.concatenate(xs,axis=1),jnp.concatenate(ts,axis=0),preferred_element_type=jnp.float32)
def gg_of(gp_ref,g):
    R=gp_ref.shape[1]//2; nb=R//16
    return jnp.concatenate([gp_ref[g,16*d:16*d+R,:] for d in range(nb)],axis=1)
def conv_bwd(gg, t):
    return lax.dot_general(gg,t,(((1,),(1,)),((),())),preferred_element_type=jnp.float32)
def filt_grad(x, gg):
    C=lax.dot_general(x,gg,(((0,),(0,)),((),())),preferred_element_type=jnp.float32)
    L=C.shape[1]
    z=jnp.zeros((H,H),jnp.float32)
    top=C[:H]; bot=jnp.concatenate([C[H:,H:],z],axis=1)
    D=top+bot
    n=H
    D=jnp.concatenate([D,z],axis=1)
    W=L+H
    lane=None
    while n>1:
        n//=2
        D=D[:n]+pltpu.roll(D[n:],W-n,1)
    return D[:,:L]


VM = pl.BlockSpec(memory_space=pltpu.VMEM)
PARAMS = pltpu.CompilerParams(vmem_limit_bytes=56 << 20)


def k_fwd(taps_ref, x_ref, y_ref, tb_ref, xp):
    G, R, _ = x_ref.shape
    xp[:, :R, :] = jnp.zeros((G, R, B), jnp.bfloat16)
    xp[:, R:, :] = x_ref[...]
    for g in range(G):
        build_tb(tb_ref, g, taps_ref[g : g + 1, :])

    def body(g, _):
        y_ref[g] = conv_fwd(xp, tb_ref, g).astype(jnp.bfloat16)
        return 0

    lax.fori_loop(0, G, body, 0)


def k_bwd(tb_ref, x_ref, g_ref, u_ref, f_ref, gp):
    G, R, _ = x_ref.shape
    gp[:, R:, :] = jnp.zeros((G, R, B), jnp.bfloat16)
    gp[:, :R, :] = g_ref[...]

    def body(g, _):
        gg = gg_of(gp, g)
        u_ref[g] = conv_bwd(gg, tmat(tb_ref, g)).astype(jnp.bfloat16)
        f_ref[g] = filt_grad(x_ref[g], gg)
        return 0

    lax.fori_loop(0, G, body, 0)


def local(query_gate, key_gate, value_input, filter_taps, out_weight, out_grad):
    length, channels = query_gate.shape
    groups = filter_taps.shape[1]
    per = channels // groups
    n = lax.axis_size("ctx")
    G = groups // n
    nb = length // B
    total = n * length
    R = n * nb * per
    scale = 1.0 / math.sqrt(total)
    f32 = jnp.float32
    bf = jnp.bfloat16

    def scatter(v):
        v = v.T.reshape(n, G * per, length)
        v = lax.all_to_all(v, "ctx", 0, 0, tiled=True)
        v = v.reshape(n, G, per, nb, B).transpose(1, 0, 3, 2, 4)
        return v.reshape(G, R, B)

    def gather(v):
        v = v.reshape(G, n, nb, per, B).transpose(1, 0, 3, 2, 4).reshape(n, G * per, length)
        v = lax.all_to_all(v, "ctx", 0, 0, tiled=True)
        return v.reshape(channels, length).T

    product_in = (key_gate.astype(f32) * value_input.astype(f32)).astype(bf)
    taps = (filter_taps * scale).T.reshape(n, G, length)
    taps = lax.all_to_all(taps, "ctx", 0, 0, tiled=True)
    taps = taps.transpose(1, 0, 2).reshape(G, total)
    x = scatter(product_in)
    y, tb = pl.pallas_call(
        k_fwd,
        in_specs=[VM] * 2,
        out_specs=(VM, VM),
        out_shape=(
            jax.ShapeDtypeStruct((G, R, B), bf),
            jax.ShapeDtypeStruct((G, H, total + 2 * H), bf),
        ),
        scratch_shapes=[pltpu.VMEM((G, 2 * R, B), bf)],
        compiler_params=PARAMS,
    )(taps, x)
    convolved = gather(y).astype(f32)
    gated_out = (query_gate.astype(f32) * convolved).astype(bf)
    partial_value = jnp.dot(gated_out, out_weight, preferred_element_type=f32)
    projected = lax.psum_scatter(partial_value.astype(bf), "tp", scatter_dimension=1, tiled=True)
    dgated = jnp.einsum(
        "tk,ck->tc",
        lax.all_gather(out_grad, "tp", axis=1, tiled=True),
        out_weight,
        preferred_element_type=f32,
    ).astype(bf).astype(f32)
    conv_grad = (dgated * query_gate.astype(f32)).astype(bf)
    gg = scatter(conv_grad)
    u, fg = pl.pallas_call(
        k_bwd,
        in_specs=[VM] * 3,
        out_specs=(VM, VM),
        out_shape=(
            jax.ShapeDtypeStruct((G, R, B), bf),
            jax.ShapeDtypeStruct((G, 1, total), f32),
        ),
        scratch_shapes=[pltpu.VMEM((G, 2 * R, B), bf)],
        compiler_params=PARAMS,
    )(tb, x, gg)
    input_grad = gather(u).astype(f32)
    fg = fg.reshape(G, n, length).transpose(1, 0, 2)
    fg = lax.all_to_all(fg, "ctx", 0, 0, tiled=True).reshape(groups, length)
    grad_filter = fg.T * scale
    grad_query = (dgated * convolved).astype(bf)
    grad_key = (input_grad * value_input.astype(f32)).astype(bf)
    grad_value = (input_grad * key_gate.astype(f32)).astype(bf)
    return (projected, grad_query, grad_key, grad_value, grad_filter)


def solution(mesh):
    spec = P("ctx", "tp")
    return jax.shard_map(
        local,
        mesh=mesh,
        in_specs=(spec, spec, spec, spec, P("tp", None), spec),
        out_specs=(spec,) * 5,
        check_vma=False,
    )
```

```python
import math

import jax
import jax.numpy as jnp
from jax import lax
from jax.experimental import pallas as pl
from jax.experimental.pallas import tpu as pltpu
from jax.sharding import PartitionSpec as P

MESH = pl.DeviceIdType.MESH
f32 = jnp.float32
bf = jnp.bfloat16
B=256; H=128
def build_tb(tb_ref, g, taps_row):
    L=taps_row.shape[1]
    z=jnp.zeros((1,H),jnp.float32)
    v=jnp.broadcast_to(jnp.concatenate([z,taps_row,z],axis=1),(16,L+2*H))
    base=pltpu.roll(v,0,1,stride=1,stride_axis=0)
    for k in range(H//16):
        r=pltpu.roll(base,16*k,1) if k else base
        tb_ref[g,16*k:16*k+16,:]=r.astype(jnp.bfloat16)
def tmat(tb_ref,g):
    L=tb_ref.shape[2]-2*H
    return jnp.concatenate([tb_ref[g,:,H:H+L],tb_ref[g,:,0:L]],axis=0)
def conv_fwd(xp_ref, tb_ref, g):
    R=xp_ref.shape[1]//2; nb=R//16
    acc=None
    xs=[xp_ref[g,R-16*d:2*R-16*d,:] for d in range(nb)]
    ts=[jnp.concatenate([tb_ref[g,:,H+B*d:H+B*d+B],tb_ref[g,:,B*d:B*d+B]],axis=0) for d in range(nb)]
    return jnp.dot(jnp.concatenate(xs,axis=1),jnp.concatenate(ts,axis=0),preferred_element_type=jnp.float32)
def gg_of(gp_ref,g):
    R=gp_ref.shape[1]//2; nb=R//16
    return jnp.concatenate([gp_ref[g,16*d:16*d+R,:] for d in range(nb)],axis=1)
def conv_bwd(gg, t):
    return lax.dot_general(gg,t,(((1,),(1,)),((),())),preferred_element_type=jnp.float32)
def filt_grad(x, gg):
    C=lax.dot_general(x,gg,(((0,),(0,)),((),())),preferred_element_type=jnp.float32)
    L=C.shape[1]
    z=jnp.zeros((H,H),jnp.float32)
    top=C[:H]; bot=jnp.concatenate([C[H:,H:],z],axis=1)
    D=top+bot
    n=H
    D=jnp.concatenate([D,z],axis=1)
    W=L+H
    lane=None
    while n>1:
        n//=2
        D=D[:n]+pltpu.roll(D[n:],W-n,1)
    return D[:,:L]


VM = pl.BlockSpec(memory_space=pltpu.VMEM)
ANY = pl.BlockSpec(memory_space=pl.ANY)
NC = 8
RA = 384
CH = 128
NA = RA // CH


def kernel(
    q_ref, k_ref, v_ref, t_ref, w_hbm, og_hbm,
    proj_ref, gq_ref, gk_ref, gv_ref, gf_ref,
    w, og, tb, xp, gp, sx, sg, yb_, ub_, yr, ur, st, rt, sf, rf,
    sp, r0, ra, rb, acc, dg, cv, go,
    lsem, ags, agr, sibs, sibr, sps, spr, ras, rar, rbs, rbr, a2s, a2r,
):
    mc = lax.axis_index("ctx")
    mt = lax.axis_index("tp")
    zh, x = mc // 4, mc % 4
    zl, y, co = mt // 8, (mt // 2) % 4, mt % 2
    yd = 1 - 2 * co
    yf, yb, yo = (y + yd + 4) % 4, (y - yd + 4) % 4, (y + 2) % 4
    zp = 1 - zl
    T = lambda z, yy: z * 8 + yy * 2 + co
    M = lambda z, yy: z * 4 + yy
    front, back = (mc, T(zl, yf)), (mc, T(zl, yb))
    zpar, sib = (mc, T(zp, y)), (mc, zl * 8 + y * 2 + 1 - co)
    peers = []
    for k in range(1, NC):
        pc = ((zh + k // 4) % 2) * 4 + (x + k % 4) % 4
        peers.append((k, pc, (pc, mt)))
    G = 4
    L = 512
    scale = 1.0 / math.sqrt(NC * L)

    barrier = pltpu.get_barrier_semaphore()
    partners = [front, back, zpar, sib] + [p[2] for p in peers]
    for d in partners:
        pl.semaphore_signal(barrier, inc=1, device_id=d, device_id_type=MESH)
    wcopy = pltpu.make_async_copy(w_hbm, w, lsem.at[0])
    wcopy.start()
    ocopy = pltpu.make_async_copy(og_hbm, og.at[mt], lsem.at[1])
    ocopy.start()

    def spread(dst, full):
        for r in range(NC):
            for g in range(G):
                for ib in range(2):
                    dst[r, g, 16 * ib : 16 * ib + 16, :] = full[
                        64 * r + 16 * g : 64 * r + 16 * g + 16, B * ib : B * ib + B
                    ]

    def joined(src):
        rows = []
        for r in range(NC):
            for g in range(G):
                rows.append(
                    jnp.concatenate([src[r, g, 0:16, :], src[r, g, 16:32, :]], axis=1)
                )
        return jnp.concatenate(rows, axis=0)

    spread(sx, (k_ref[...].astype(f32) * v_ref[...].astype(f32)).astype(bf).T)
    tt = (t_ref[...] * scale).T
    for r in range(NC):
        st[r, 0:G, :] = tt[G * r : G * r + G, :]
        st[r, G:8, :] = tt[G * r : G * r + G, :]
    pl.semaphore_wait(barrier, len(partners))

    def rc(src, dst, s, r, dev):
        c = pltpu.make_async_remote_copy(
            src_ref=src, dst_ref=dst, send_sem=s, recv_sem=r, device_id=dev, device_id_type=MESH
        )
        c.start()
        return c

    sent = []

    def ag(i, z, yy, lo, n, dev, src=None):
        slot = T(z, yy)
        if src is None:
            s = og.at[slot, pl.ds(lo, n), :]
        else:
            s = src.at[pl.ds(lo, n), :]
        c = rc(s, og.at[slot, pl.ds(lo, n), :], ags.at[i], agr.at[i], dev)
        sent.append(c)
        return c

    RB = L - RA
    m1 = ag(0, zl, y, RA, RB, front, og_hbm)
    m2 = ag(1, zl, y, RA, RB, back, og_hbm)
    m3 = ag(2, zl, y, 0, RA, front, og_hbm)
    m4 = ag(3, zl, y, 0, RA, back, og_hbm)

    def a2a(base, src, dst):
        out = []
        for k, pc, dev in peers:
            c = rc(src(pc), dst, a2s.at[base, k - 1], a2r.at[base, k - 1], dev)
            sent.append(c)
            out.append(c)
        return out

    at32 = lambda c, off: pl.ds(pl.multiple_of(32 * c + off, 32), 32)
    tcs = a2a(0, lambda pc: st.at[pc], rt.at[mc])
    xcs = a2a(1, lambda pc: sx.at[pc], xp.at[:, at32(mc, B), :])
    m5 = ag(4, zl, y, 0, RA, zpar, og_hbm)
    m6 = ag(5, zl, y, RA, RB, zpar, og_hbm)

    def sibsend(z, yy, src=None):
        slot = T(z, yy)
        m = M(z, yy)
        c = rc(og.at[slot] if src is None else src, og.at[slot], sibs.at[m], sibr.at[m], sib)
        sent.append(c)
        return c

    def sibwait(z, yy):
        slot = z * 8 + yy * 2 + 1 - co
        m = M(z, yy)
        pltpu.make_async_remote_copy(
            src_ref=og.at[slot], dst_ref=og.at[slot], send_sem=sibs.at[m], recv_sem=sibr.at[m],
            device_id=sib, device_id_type=MESH,
        ).wait_recv()

    sibsend(zl, y, og_hbm)

    xp[:, 0:B, :] = jnp.zeros((G, B, B), bf)
    gp[:, B : 2 * B, :] = jnp.zeros((G, B, B), bf)
    xp[:, at32(mc, B), :] = sx[mc]
    rt[mc] = st[mc]
    acc[...] = jnp.zeros(acc.shape, f32)

    m1.wait_recv()
    m7 = ag(6, zl, yb, RA, RB, front)
    m8 = ag(7, zl, yb, RA, RB, zpar)
    m2.wait_recv()
    m9 = ag(8, zl, yf, RA, RB, zpar)

    for c in tcs:
        c.wait_recv()
    for g in range(G):
        build_tb(tb, g, jnp.concatenate([rt[s, g : g + 1, :] for s in range(NC)], axis=1))
    m7.wait_recv()
    m10 = ag(9, zl, yo, RA, RB, zpar)
    m5.wait_recv()
    m11 = ag(10, zp, y, 0, RA, front)
    m12 = ag(11, zp, y, 0, RA, back)
    for c in xcs:
        c.wait_recv()

    def fwd(g, _):
        yb_[g] = conv_fwd(xp, tb, g).astype(bf)
        return 0

    lax.fori_loop(0, G, fwd, 0)
    ycs = a2a(2, lambda pc: yb_.at[:, at32(pc, 0), :], yr.at[mc])
    yr[mc] = yb_[:, at32(mc, 0), :]

    m3.wait_recv()
    m13 = ag(12, zl, yb, 0, RA, front)
    sibsend(zl, yb)
    m4.wait_recv()
    sibsend(zl, yf)

    wcopy.wait()
    ocopy.wait()

    def dstep(z, yy):
        sibwait(z, yy)
        m = M(z, yy)

        def half(h, _):
            rows = pl.ds(pl.multiple_of(h * B, B), B)
            nt = (((1,), (1,)), ((), ()))
            a = lax.dot_general(
                og[2 * m, rows, :], w[:, pl.ds(pl.multiple_of(m * 1024, 1024), 512)],
                nt, preferred_element_type=f32,
            )
            b = lax.dot_general(
                og[2 * m + 1, rows, :], w[:, pl.ds(pl.multiple_of(m * 1024 + 512, 512), 512)],
                nt, preferred_element_type=f32,
            )
            acc[rows, :] += a + b
            return 0

        lax.fori_loop(0, 2, half, 0)

    dstep(zl, y)
    m6.wait_recv()
    sibsend(zp, y)
    dstep(zl, yb)
    dstep(zl, yf)
    dstep(zp, y)

    for c in ycs:
        c.wait_recv()
    conv = joined(yr).T
    cv[...] = conv
    go[...] = (q_ref[...].astype(f32) * conv.astype(f32)).astype(bf)

    def psib(o, _):
        z = (zl + o % 2) % 2
        yy = (y + 2 + o // 2) % 4
        m = M(z, yy)
        cols = pl.ds(pl.multiple_of((2 * m + 1 - co) * 512, 512), 512)
        sp[m] = jnp.dot(go[...], w[:, cols], preferred_element_type=f32).astype(bf)
        rc(sp.at[m], r0.at[m], sps.at[m], spr.at[m], sib)
        return 0

    lax.fori_loop(0, 8, psib, 0)

    m11.wait_recv()
    m14 = ag(13, zp, yb, 0, RA, front)
    m8.wait_recv()
    sibsend(zp, yb)
    m12.wait_recv()
    m9.wait_recv()
    sibsend(zp, yf)
    m13.wait_recv()
    sibsend(zl, yo)
    dstep(zp, yb)
    dstep(zp, yf)
    dstep(zl, yo)

    def spdesc(m):
        return pltpu.make_async_remote_copy(
            src_ref=sp.at[m], dst_ref=r0.at[m], send_sem=sps.at[m], recv_sem=spr.at[m],
            device_id=sib, device_id_type=MESH,
        )

    def own(yy):
        def one(o, _):
            m = M((zl + o) % 2, yy)
            cols = pl.ds(pl.multiple_of((2 * m + co) * 512, 512), 512)
            spdesc(m).wait_recv()
            r0[m] = (
                jnp.dot(go[...], w[:, cols], preferred_element_type=f32) + r0[m].astype(f32)
            ).astype(bf)
            return 0

        lax.fori_loop(0, 2, one, 0)

    def sa(i, j, z, yy, dev):
        c = rc(r0.at[M(z, yy), pl.ds(CH * j, CH), :], ra.at[i, j], ras.at[i, j], rar.at[i, j], dev)
        sent.append(c)
        return c

    def sb(i, z, yy, dev):
        c = rc(r0.at[M(z, yy), pl.ds(RA, RB), :], rb.at[i], rbs.at[i], rbr.at[i], dev)
        sent.append(c)
        return c

    def add(z, yy, lo, n, *parts):
        rows = pl.ds(lo, n)
        m = M(z, yy)
        total = r0[m, rows, :].astype(f32)
        for p in parts:
            total = total + p.astype(f32)
        return total

    own(yo)
    b1 = sb(0, zp, yo, zpar)
    a1 = [sa(0, j, zl, yo, front) for j in range(NA)]
    a2 = [sa(1, j, zp, yo, front) for j in range(NA)]
    own(yb)
    b2 = sb(1, zp, yb, zpar)
    a3 = [sa(2, j, zl, yb, back) for j in range(NA)]
    a4 = [sa(3, j, zp, yb, back) for j in range(NA)]
    own(yf)
    b3 = sb(2, zp, yf, zpar)
    own(y)
    b4 = sb(3, zp, y, zpar)

    m14.wait_recv()
    m10.wait_recv()
    sibsend(zp, yo)
    dstep(zp, yo)
    dgv = acc[...].astype(bf)
    dg[...] = dgv
    spread(sg, (dgv.astype(f32) * q_ref[...].astype(f32)).astype(bf).T)
    gcs = a2a(3, lambda pc: sg.at[pc], gp.at[:, at32(mc, 0), :])
    gp[:, at32(mc, 0), :] = sg[mc]
    gq_ref[...] = (dg[...].astype(f32) * cv[...].astype(f32)).astype(bf)

    a5, a6, a7 = [], [], []
    for j in range(NA):
        a1[j].wait_recv()
        r0[M(zl, yf), pl.ds(CH * j, CH), :] = add(zl, yf, CH * j, CH, ra[0, j]).astype(bf)
        a5.append(sa(4, j, zl, yf, front))
    b1.wait_recv()
    r0[M(zl, yo), pl.ds(RA, RB), :] = add(zl, yo, RA, RB, rb[0]).astype(bf)
    b5 = sb(4, zl, yo, front)
    for j in range(NA):
        a2[j].wait_recv()
        r0[M(zp, yf), pl.ds(CH * j, CH), :] = add(zp, yf, CH * j, CH, ra[1, j]).astype(bf)
        a6.append(sa(5, j, zp, yf, front))
    b2.wait_recv()
    r0[M(zl, yb), pl.ds(RA, RB), :] = add(zl, yb, RA, RB, rb[1]).astype(bf)
    b6 = sb(5, zl, yb, back)

    for c in gcs:
        c.wait_recv()

    def bwd(g, _):
        ub_[g] = conv_bwd(gg_of(gp, g), tmat(tb, g)).astype(bf)
        return 0

    lax.fori_loop(0, G, bwd, 0)
    ucs = a2a(4, lambda pc: ub_.at[:, at32(pc, 0), :], ur.at[mc])
    ur[mc] = ub_[:, at32(mc, 0), :]

    b3.wait_recv()
    b5.wait_recv()
    r0[M(zl, yf), pl.ds(RA, RB), :] = add(zl, yf, RA, RB, rb[2], rb[4]).astype(bf)
    b7 = sb(6, zl, yf, front)

    for g in range(G):
        row = filt_grad(xp[g, B : 2 * B, :], gg_of(gp, g)) * scale
        for r in range(NC):
            sf[r, g : g + 1, :] = row[:, L * r : L * r + L]
            sf[r, G + g : G + g + 1, :] = row[:, L * r : L * r + L]
    fcs = a2a(5, lambda pc: sf.at[pc], rf.at[mc])
    rf[mc] = sf[mc]

    for j in range(NA):
        a4[j].wait_recv()
        a6[j].wait_recv()
        r0[M(zp, y), pl.ds(CH * j, CH), :] = add(zp, y, CH * j, CH, ra[3, j], ra[5, j]).astype(bf)
        a7.append(sa(6, j, zp, y, zpar))

    for c in ucs:
        c.wait_recv()
    u = joined(ur).T.astype(f32)
    gk_ref[...] = (u * v_ref[...].astype(f32)).astype(bf)
    gv_ref[...] = (u * k_ref[...].astype(f32)).astype(bf)
    for c in fcs:
        c.wait_recv()
    gf_ref[...] = jnp.concatenate([rf[s, 0:G, :] for s in range(NC)], axis=0).T

    b4.wait_recv()
    b6.wait_recv()
    b7.wait_recv()
    proj_ref[pl.ds(RA, RB), :] = add(zl, y, RA, RB, rb[3], rb[5], rb[6]).astype(bf)
    for j in range(NA):
        a3[j].wait_recv()
        a5[j].wait_recv()
        a7[j].wait_recv()
        proj_ref[pl.ds(CH * j, CH), :] = add(
            zl, y, CH * j, CH, ra[2, j], ra[4, j], ra[6, j]
        ).astype(bf)

    for c in sent:
        c.wait_send()

    def drain(m, _):
        spdesc(m).wait_send()
        return 0

    lax.fori_loop(0, 8, drain, 0)


def local(query_gate, key_gate, value_input, filter_taps, out_weight, out_grad):
    L, D = query_gate.shape
    G = 4
    blk = jax.ShapeDtypeStruct((L, D), bf)
    vm = pltpu.VMEM
    dma = pltpu.SemaphoreType.DMA
    return pl.pallas_call(
        kernel,
        in_specs=[VM, VM, VM, VM, ANY, ANY],
        out_specs=(VM,) * 5,
        out_shape=(blk, blk, blk, blk, jax.ShapeDtypeStruct(filter_taps.shape, f32)),
        scratch_shapes=[
            vm(out_weight.shape, bf),
            vm((16, L, D), bf),
            vm((G, H, NC * L + 2 * H), bf),
            vm((G, 2 * B, B), bf),
            vm((G, 2 * B, B), bf),
            vm((NC, G, 32, B), bf),
            vm((NC, G, 32, B), bf),
            vm((G, B, B), bf),
            vm((G, B, B), bf),
            vm((NC, G, 32, B), bf),
            vm((NC, G, 32, B), bf),
            vm((NC, 8, L), f32),
            vm((NC, 8, L), f32),
            vm((NC, 8, L), f32),
            vm((NC, 8, L), f32),
            vm((8, L, D), bf),
            vm((8, L, D), bf),
            vm((7, NA, CH, D), bf),
            vm((7, L - RA, D), bf),
            vm((L, D), f32),
            vm((L, D), bf),
            vm((L, D), bf),
            vm((L, D), bf),
            dma((2,)),
            dma((14,)), dma((14,)),
            dma((8,)), dma((8,)),
            dma((8,)), dma((8,)),
            dma((7, NA)), dma((7, NA)),
            dma((7,)), dma((7,)),
            dma((6, NC - 1)), dma((6, NC - 1)),
        ],
        compiler_params=pltpu.CompilerParams(
            collective_id=0, has_side_effects=True, vmem_limit_bytes=62 << 20
        ),
        name="hyena",
    )(query_gate, key_gate, value_input, filter_taps, out_weight, out_grad)


def solution(mesh):
    spec = P("ctx", "tp")
    return jax.shard_map(
        local,
        mesh=mesh,
        in_specs=(spec, spec, spec, spec, P("tp", None), spec),
        out_specs=(spec,) * 5,
        check_vma=False,
    )
```

```python
import math

import jax
import jax.numpy as jnp
from jax import lax
from jax.experimental import pallas as pl
from jax.experimental.pallas import tpu as pltpu
from jax.sharding import PartitionSpec as P

MESH = pl.DeviceIdType.MESH
f32 = jnp.float32
bf = jnp.bfloat16
B=256; H=128
def build_tb(tb_ref, g, taps_row):
    L=taps_row.shape[1]
    z=jnp.zeros((1,H),jnp.float32)
    v=jnp.broadcast_to(jnp.concatenate([z,taps_row,z],axis=1),(16,L+2*H))
    base=pltpu.roll(v,0,1,stride=1,stride_axis=0)
    for k in range(H//16):
        r=pltpu.roll(base,16*k,1) if k else base
        tb_ref[g,16*k:16*k+16,:]=r.astype(jnp.bfloat16)
def tmat(tb_ref,g):
    L=tb_ref.shape[2]-2*H
    return jnp.concatenate([tb_ref[g,:,H:H+L],tb_ref[g,:,0:L]],axis=0)
def conv_fwd(xp_ref, tb_ref, g):
    R=xp_ref.shape[1]//2; nb=R//16
    acc=None
    xs=[xp_ref[g,R-16*d:2*R-16*d,:] for d in range(nb)]
    ts=[jnp.concatenate([tb_ref[g,:,H+B*d:H+B*d+B],tb_ref[g,:,B*d:B*d+B]],axis=0) for d in range(nb)]
    return jnp.dot(jnp.concatenate(xs,axis=1),jnp.concatenate(ts,axis=0),preferred_element_type=jnp.float32)
def gg_of(gp_ref,g):
    R=gp_ref.shape[1]//2; nb=R//16
    return jnp.concatenate([gp_ref[g,16*d:16*d+R,:] for d in range(nb)],axis=1)
def conv_bwd(gg, t):
    return lax.dot_general(gg,t,(((1,),(1,)),((),())),preferred_element_type=jnp.float32)
def filt_grad(x, gg):
    C=lax.dot_general(x,gg,(((0,),(0,)),((),())),preferred_element_type=jnp.float32)
    L=C.shape[1]
    z=jnp.zeros((H,H),jnp.float32)
    top=C[:H]; bot=jnp.concatenate([C[H:,H:],z],axis=1)
    D=top+bot
    n=H
    D=jnp.concatenate([D,z],axis=1)
    W=L+H
    lane=None
    while n>1:
        n//=2
        D=D[:n]+pltpu.roll(D[n:],W-n,1)
    return D[:,:L]


VM = pl.BlockSpec(memory_space=pltpu.VMEM)
ANY = pl.BlockSpec(memory_space=pl.ANY)
NC = 8
RA = 384
CH = 128
NA = RA // CH


def kernel(
    q_hbm, k_hbm, v_hbm, t_hbm, w_hbm, og_hbm,
    proj_out, gq_out, gk_out, gv_out, gf_out,
    w, og, tb, xp, gp, sx, sg, yb_, ub_, yr, ur, st, rt, sf, rf,
    sp, r0, ra, rb, acc, dg, cv, go, q_ref, k_ref, v_ref, t_ref,
    proj_ref, gq_ref, gk_ref, gv_ref, gf_ref,
    lsem, osem, ags, agr, sibs, sibr, sps, spr, ras, rar, rbs, rbr, a2s, a2r,
):
    mc = lax.axis_index("ctx")
    mt = lax.axis_index("tp")
    zh, x = mc // 4, mc % 4
    zl, y, co = mt // 8, (mt // 2) % 4, mt % 2
    yd = 1 - 2 * co
    yf, yb, yo = (y + yd + 4) % 4, (y - yd + 4) % 4, (y + 2) % 4
    zp = 1 - zl
    T = lambda z, yy: z * 8 + yy * 2 + co
    M = lambda z, yy: z * 4 + yy
    front, back = (mc, T(zl, yf)), (mc, T(zl, yb))
    zpar, sib = (mc, T(zp, y)), (mc, zl * 8 + y * 2 + 1 - co)
    peers = []
    for k in range(1, NC):
        pc = ((zh + k // 4) % 2) * 4 + (x + k % 4) % 4
        peers.append((k, pc, (pc, mt)))
    G = 4
    L = 512
    RB = L - RA
    scale = 1.0 / math.sqrt(NC * L)

    barrier = pltpu.get_barrier_semaphore()
    partners = [front, back, zpar, sib] + [p[2] for p in peers]
    for d in partners:
        pl.semaphore_signal(barrier, inc=1, device_id=d, device_id_type=MESH)

    def lc(src, dst, sem):
        c = pltpu.make_async_copy(src, dst, sem)
        c.start()
        return c

    tcopy = lc(t_hbm, t_ref, lsem.at[0])
    kcopy = lc(k_hbm, k_ref, lsem.at[1])
    vcopy = lc(v_hbm, v_ref, lsem.at[2])
    qcopy = lc(q_hbm, q_ref, lsem.at[3])
    ocopy = lc(og_hbm, og.at[mt], lsem.at[4])
    wcopy = lc(w_hbm, w, lsem.at[5])

    def spread(dst, full):
        for r in range(NC):
            for g in range(G):
                for ib in range(2):
                    dst[r, g, 16 * ib : 16 * ib + 16, :] = full[
                        64 * r + 16 * g : 64 * r + 16 * g + 16, B * ib : B * ib + B
                    ]

    def joined(src):
        rows = []
        for r in range(NC):
            for g in range(G):
                rows.append(
                    jnp.concatenate([src[r, g, 0:16, :], src[r, g, 16:32, :]], axis=1)
                )
        return jnp.concatenate(rows, axis=0)

    def rc(src, dst, s, r, dev):
        c = pltpu.make_async_remote_copy(
            src_ref=src, dst_ref=dst, send_sem=s, recv_sem=r, device_id=dev, device_id_type=MESH
        )
        c.start()
        return c

    sent = []

    def ag(i, z, yy, lo, n, dev, src=None, j=0):
        slot = T(z, yy)
        if src is None:
            s = og.at[slot, pl.ds(lo, n), :]
        else:
            s = src.at[pl.ds(lo, n), :]
        c = rc(s, og.at[slot, pl.ds(lo, n), :], ags.at[i, j], agr.at[i, j], dev)
        sent.append(c)
        return c

    def aga(i, z, yy, dev, j, src=None):
        return ag(i, z, yy, CH * j, CH, dev, src, j)

    def agb(i, z, yy, dev, src=None):
        return ag(i, z, yy, RA, RB, dev, src)

    def a2a(base, src, dst):
        out = []
        for k, pc, dev in peers:
            c = rc(src(pc), dst, a2s.at[base, k - 1], a2r.at[base, k - 1], dev)
            sent.append(c)
            out.append(c)
        return out

    def recv(cs):
        for c in cs:
            c.wait_recv()

    at32 = lambda c, off: pl.ds(pl.multiple_of(32 * c + off, 32), 32)
    hf = lambda h: pl.ds(2 * h, 2)

    def sibsend(z, yy, src=None):
        slot = T(z, yy)
        m = M(z, yy)
        c = rc(og.at[slot] if src is None else src, og.at[slot], sibs.at[m], sibr.at[m], sib)
        sent.append(c)
        return c

    def sibwait(z, yy):
        slot = z * 8 + yy * 2 + 1 - co
        m = M(z, yy)
        pltpu.make_async_remote_copy(
            src_ref=og.at[slot], dst_ref=og.at[slot], send_sem=sibs.at[m], recv_sem=sibr.at[m],
            device_id=sib, device_id_type=MESH,
        ).wait_recv()

    pl.semaphore_wait(barrier, len(partners))
    J = range(NA)
    m5 = [aga(4, zl, y, zpar, 0, og_hbm)]
    m1 = agb(0, zl, y, front, og_hbm)
    m2 = agb(1, zl, y, back, og_hbm)
    m3 = [aga(2, zl, y, front, j, og_hbm) for j in J]
    m4 = [aga(3, zl, y, back, j, og_hbm) for j in J]
    tcopy.wait()
    for r in range(NC):
        blk = t_ref[G * r : G * r + G, :] * scale
        st[r, 0:G, :] = blk
        st[r, G:8, :] = blk
    tcs = a2a(0, lambda pc: st.at[pc], rt.at[mc])
    kcopy.wait()
    vcopy.wait()
    spread(sx, (k_ref[...].astype(f32) * v_ref[...].astype(f32)).astype(bf).T)
    xcs = [
        a2a(1 + h, lambda pc, h=h: sx.at[pc, hf(h)], xp.at[hf(h), at32(mc, B), :]) for h in (0, 1)
    ]
    for j in range(1, NA):
        m5.append(aga(4, zl, y, zpar, j, og_hbm))
    sibsend(zl, y, og_hbm)

    xp[:, 0:B, :] = jnp.zeros((G, B, B), bf)
    gp[:, B : 2 * B, :] = jnp.zeros((G, B, B), bf)
    xp[:, at32(mc, B), :] = sx[mc]
    rt[mc] = st[mc]
    acc[...] = jnp.zeros(acc.shape, f32)

    m5[0].wait_recv()
    m11 = [aga(10, zp, y, front, 0)]
    m12 = [aga(11, zp, y, back, 0)]
    m1.wait_recv()
    m7 = agb(6, zl, yb, front)
    recv(tcs)
    for g in range(G):
        build_tb(tb, g, jnp.concatenate([rt[s, g : g + 1, :] for s in range(NC)], axis=1))

    def fwd(g, _):
        yb_[g] = conv_fwd(xp, tb, g).astype(bf)
        return 0

    ycs = []
    for h in (0, 1):
        recv(xcs[h])
        lax.fori_loop(2 * h, 2 * h + 2, fwd, 0)
        ycs.append(
            a2a(3 + h, lambda pc, h=h: yb_.at[hf(h), at32(pc, 0), :], yr.at[mc, hf(h)])
        )
        if h == 0:
            for j in range(1, NA):
                m5[j].wait_recv()
                m11.append(aga(10, zp, y, front, j))
                m12.append(aga(11, zp, y, back, j))
    yr[mc] = yb_[:, at32(mc, 0), :]
    m6 = agb(5, zl, y, zpar, og_hbm)
    m8 = agb(7, zl, yb, zpar)
    m2.wait_recv()
    m9 = agb(8, zl, yf, zpar)

    m13 = []
    for j in J:
        m3[j].wait_recv()
        m13.append(aga(12, zl, yb, front, j))
    sibsend(zl, yb)
    recv(m4)
    sibsend(zl, yf)

    wcopy.wait()
    ocopy.wait()
    qcopy.wait()

    def dstep(z, yy):
        sibwait(z, yy)
        m = M(z, yy)

        def half(h, _):
            rows = pl.ds(pl.multiple_of(h * B, B), B)
            nt = (((1,), (1,)), ((), ()))
            a = lax.dot_general(
                og[2 * m, rows, :], w[:, pl.ds(pl.multiple_of(m * 1024, 1024), 512)],
                nt, preferred_element_type=f32,
            )
            b = lax.dot_general(
                og[2 * m + 1, rows, :], w[:, pl.ds(pl.multiple_of(m * 1024 + 512, 512), 512)],
                nt, preferred_element_type=f32,
            )
            acc[rows, :] += a + b
            return 0

        lax.fori_loop(0, 2, half, 0)

    dstep(zl, y)
    m7.wait_recv()
    m10 = agb(9, zl, yo, zpar)
    m14 = [None] * NA
    for j in range(NA - 1):
        m11[j].wait_recv()
        m14[j] = aga(13, zp, yb, front, j)
    dstep(zl, yb)
    dstep(zl, yf)

    recv(ycs[0])
    recv(ycs[1])
    conv = joined(yr).T
    cv[...] = conv
    go[...] = (q_ref[...].astype(f32) * conv.astype(f32)).astype(bf)

    def psib(o, _):
        z = (zp + o % 2) % 2
        yy = (y + 2 + o // 2) % 4
        m = M(z, yy)
        cols = pl.ds(pl.multiple_of((2 * m + 1 - co) * 512, 512), 512)
        sp[m] = jnp.dot(go[...], w[:, cols], preferred_element_type=f32).astype(bf)
        rc(sp.at[m], r0.at[m], sps.at[m], spr.at[m], sib)
        return 0

    lax.fori_loop(0, 4, psib, 0)
    m11[NA - 1].wait_recv()
    m14[NA - 1] = aga(13, zp, yb, front, NA - 1)
    m6.wait_recv()
    sibsend(zp, y)
    lax.fori_loop(4, 8, psib, 0)

    def spdesc(m):
        return pltpu.make_async_remote_copy(
            src_ref=sp.at[m], dst_ref=r0.at[m], send_sem=sps.at[m], recv_sem=spr.at[m],
            device_id=sib, device_id_type=MESH,
        )

    def own(yy):
        def one(o, _):
            m = M((zp + o) % 2, yy)
            cols = pl.ds(pl.multiple_of((2 * m + co) * 512, 512), 512)
            spdesc(m).wait_recv()
            r0[m] = (
                jnp.dot(go[...], w[:, cols], preferred_element_type=f32) + r0[m].astype(f32)
            ).astype(bf)
            return 0

        lax.fori_loop(0, 2, one, 0)

    def sa(i, j, z, yy, dev):
        c = rc(r0.at[M(z, yy), pl.ds(CH * j, CH), :], ra.at[i, j], ras.at[i, j], rar.at[i, j], dev)
        sent.append(c)
        return c

    def sb(i, z, yy, dev):
        c = rc(r0.at[M(z, yy), pl.ds(RA, RB), :], rb.at[i], rbs.at[i], rbr.at[i], dev)
        sent.append(c)
        return c

    def add(z, yy, lo, n, *parts):
        rows = pl.ds(lo, n)
        m = M(z, yy)
        total = r0[m, rows, :].astype(f32)
        for p in parts:
            total = total + p.astype(f32)
        return total

    def put(z, yy, lo, n, *parts):
        r0[M(z, yy), pl.ds(lo, n), :] = add(z, yy, lo, n, *parts).astype(bf)

    own(yo)
    a2 = [sa(1, j, zp, yo, front) for j in J]
    b1 = sb(0, zp, yo, zpar)
    m8.wait_recv()
    sibsend(zp, yb)
    m9.wait_recv()
    recv(m12)
    sibsend(zp, yf)
    own(yb)
    a4 = [sa(3, j, zp, yb, back) for j in J]
    b2 = sb(1, zp, yb, zpar)
    recv(m13)
    sibsend(zl, yo)
    dstep(zp, y)
    dstep(zp, yb)
    dstep(zp, yf)
    own(yf)
    b3 = sb(2, zp, yf, zpar)
    dstep(zl, yo)
    recv(m14)
    m10.wait_recv()
    sibsend(zp, yo)
    own(y)
    b4 = sb(3, zp, y, zpar)
    dstep(zp, yo)
    dgv = acc[...].astype(bf)
    dg[...] = dgv
    spread(sg, (dgv.astype(f32) * q_ref[...].astype(f32)).astype(bf).T)
    gcs = [
        a2a(5 + h, lambda pc, h=h: sg.at[pc, hf(h)], gp.at[hf(h), at32(mc, 0), :]) for h in (0, 1)
    ]
    a1 = [sa(0, j, zl, yo, front) for j in J]
    gp[:, at32(mc, 0), :] = sg[mc]
    gq_ref[...] = (dg[...].astype(f32) * cv[...].astype(f32)).astype(bf)
    outs = [lc(gq_ref, gq_out, osem.at[0])]

    a5, a6, a7 = [], [], []
    for j in J:
        a2[j].wait_recv()
        put(zp, yf, CH * j, CH, ra[1, j])
        a6.append(sa(5, j, zp, yf, front))
    a3 = [sa(2, j, zl, yb, back) for j in J]
    b1.wait_recv()
    put(zl, yo, RA, RB, rb[0])
    b5 = sb(4, zl, yo, front)
    b2.wait_recv()
    put(zl, yb, RA, RB, rb[1])
    b6 = sb(5, zl, yb, back)

    def bwd(g, _):
        ub_[g] = conv_bwd(gg_of(gp, g), tmat(tb, g)).astype(bf)
        return 0

    def fgrad(g):
        row = filt_grad(xp[g, B : 2 * B, :], gg_of(gp, g)) * scale
        for r in range(NC):
            sf[r, g : g + 1, :] = row[:, L * r : L * r + L]
            sf[r, G + g : G + g + 1, :] = row[:, L * r : L * r + L]

    ucs = []
    for h in (0, 1):
        recv(gcs[h])
        lax.fori_loop(2 * h, 2 * h + 2, bwd, 0)
        ucs.append(
            a2a(7 + h, lambda pc, h=h: ub_.at[hf(h), at32(pc, 0), :], ur.at[mc, hf(h)])
        )
    ur[mc] = ub_[:, at32(mc, 0), :]
    fgrad(0)
    for j in J:
        a1[j].wait_recv()
        put(zl, yf, CH * j, CH, ra[0, j])
        a5.append(sa(4, j, zl, yf, front))
    b3.wait_recv()
    b5.wait_recv()
    put(zl, yf, RA, RB, rb[2], rb[4])
    b7 = sb(6, zl, yf, front)
    fgrad(1)
    for j in J:
        a4[j].wait_recv()
        a6[j].wait_recv()
        put(zp, y, CH * j, CH, ra[3, j], ra[5, j])
        a7.append(sa(6, j, zp, y, zpar))
    fgrad(2)
    fgrad(3)
    fcs = a2a(9, lambda pc: sf.at[pc], rf.at[mc])
    rf[mc] = sf[mc]

    recv(ucs[0])
    recv(ucs[1])
    u = joined(ur).T.astype(f32)
    gk_ref[...] = (u * v_ref[...].astype(f32)).astype(bf)
    outs.append(lc(gk_ref, gk_out, osem.at[1]))
    gv_ref[...] = (u * k_ref[...].astype(f32)).astype(bf)
    outs.append(lc(gv_ref, gv_out, osem.at[2]))
    recv(fcs)
    for s in range(NC):
        gf_ref[G * s : G * s + G, :] = rf[s, 0:G, :]
    outs.append(lc(gf_ref, gf_out, osem.at[3]))

    for j in J:
        a3[j].wait_recv()
        a7[j].wait_recv()
        a5[j].wait_recv()
        proj_ref[pl.ds(CH * j, CH), :] = add(
            zl, y, CH * j, CH, ra[2, j], ra[4, j], ra[6, j]
        ).astype(bf)
    b4.wait_recv()
    b6.wait_recv()
    b7.wait_recv()
    proj_ref[pl.ds(RA, RB), :] = add(zl, y, RA, RB, rb[3], rb[5], rb[6]).astype(bf)
    outs.append(lc(proj_ref, proj_out, osem.at[4]))

    for c in sent:
        c.wait_send()

    def drain(m, _):
        spdesc(m).wait_send()
        return 0

    lax.fori_loop(0, 8, drain, 0)
    for c in outs:
        c.wait()


def handover(*refs):
    n = 5
    ins, outs, held, sem = refs[:n], refs[n : 2 * n], refs[2 * n : 3 * n], refs[-1]
    first = [pltpu.make_async_copy(ins[i], held[i], sem.at[0, i]) for i in range(n)]
    then = [pltpu.make_async_copy(held[i], outs[i], sem.at[1, i]) for i in range(n)]
    for c in first:
        c.start()
    for i in range(n):
        first[i].wait()
        then[i].start()
    for c in then:
        c.wait()


def local(query_gate, key_gate, value_input, filter_taps, out_weight, out_grad):
    L, D = query_gate.shape
    G = 4
    blk = jax.ShapeDtypeStruct((L, D), bf)
    vm = pltpu.VMEM
    dma = pltpu.SemaphoreType.DMA
    shapes = (blk, blk, blk, blk, jax.ShapeDtypeStruct(filter_taps.shape[::-1], f32))
    parts = pl.pallas_call(
        kernel,
        in_specs=[ANY] * 6,
        out_specs=(ANY,) * 5,
        out_shape=shapes,
        scratch_shapes=[
            vm(out_weight.shape, bf),
            vm((16, L, D), bf),
            vm((G, H, NC * L + 2 * H), bf),
            vm((G, 2 * B, B), bf),
            vm((G, 2 * B, B), bf),
            vm((NC, G, 32, B), bf),
            vm((NC, G, 32, B), bf),
            vm((G, B, B), bf),
            vm((G, B, B), bf),
            vm((NC, G, 32, B), bf),
            vm((NC, G, 32, B), bf),
            vm((NC, 8, L), f32),
            vm((NC, 8, L), f32),
            vm((NC, 8, L), f32),
            vm((NC, 8, L), f32),
            vm((8, L, D), bf),
            vm((8, L, D), bf),
            vm((7, NA, CH, D), bf),
            vm((7, L - RA, D), bf),
            vm((L, D), f32),
            vm((L, D), bf),
            vm((L, D), bf),
            vm((L, D), bf),
            vm((L, D), bf),
            vm((L, D), bf),
            vm((L, D), bf),
            vm((filter_taps.shape[1], L), f32),
            vm((L, D), bf),
            vm((L, D), bf),
            vm((L, D), bf),
            vm((L, D), bf),
            vm((filter_taps.shape[1], L), f32),
            dma((6,)), dma((5,)),
            dma((14, NA)), dma((14, NA)),
            dma((8,)), dma((8,)),
            dma((8,)), dma((8,)),
            dma((7, NA)), dma((7, NA)),
            dma((7,)), dma((7,)),
            dma((10, NC - 1)), dma((10, NC - 1)),
        ],
        compiler_params=pltpu.CompilerParams(
            collective_id=0, has_side_effects=True, vmem_limit_bytes=62 << 20
        ),
        name="hyena",
    )(query_gate, key_gate, value_input, filter_taps.T, out_weight, out_grad)
    done = pl.pallas_call(
        handover,
        in_specs=[ANY] * 5,
        out_specs=(ANY,) * 5,
        out_shape=shapes,
        scratch_shapes=[vm(a.shape, a.dtype) for a in shapes] + [dma((2, 5))],
        name="handover",
    )(*parts)
    return (*done[:4], done[4].T)


def solution(mesh):
    spec = P("ctx", "tp")
    return jax.shard_map(
        local,
        mesh=mesh,
        in_specs=(spec, spec, spec, spec, P("tp", None), spec),
        out_specs=(spec,) * 5,
        check_vma=False,
    )
```

```python
import math

import jax
import jax.numpy as jnp
from jax import lax
from jax.experimental import pallas as pl
from jax.experimental.pallas import tpu as pltpu
from jax.sharding import PartitionSpec as P

MESH = pl.DeviceIdType.MESH
f32 = jnp.float32
bf = jnp.bfloat16
B=256; H=128
def build_tb(tb_ref, g, taps_row):
    L=taps_row.shape[1]
    z=jnp.zeros((1,H),jnp.float32)
    v=jnp.broadcast_to(jnp.concatenate([z,taps_row,z],axis=1),(16,L+2*H))
    base=pltpu.roll(v,0,1,stride=1,stride_axis=0)
    for k in range(H//16):
        r=pltpu.roll(base,16*k,1) if k else base
        tb_ref[g,16*k:16*k+16,:]=r.astype(jnp.bfloat16)
def tmat(tb_ref,g):
    L=tb_ref.shape[2]-2*H
    return jnp.concatenate([tb_ref[g,:,H:H+L],tb_ref[g,:,0:L]],axis=0)
def conv_fwd(xp_ref, tb_ref, g):
    R=xp_ref.shape[1]//2; nb=R//16
    acc=None
    xs=[xp_ref[g,R-16*d:2*R-16*d,:] for d in range(nb)]
    ts=[jnp.concatenate([tb_ref[g,:,H+B*d:H+B*d+B],tb_ref[g,:,B*d:B*d+B]],axis=0) for d in range(nb)]
    return jnp.dot(jnp.concatenate(xs,axis=1),jnp.concatenate(ts,axis=0),preferred_element_type=jnp.float32)
def gg_of(gp_ref,g):
    R=gp_ref.shape[1]//2; nb=R//16
    return jnp.concatenate([gp_ref[g,16*d:16*d+R,:] for d in range(nb)],axis=1)
def conv_bwd(gg, t):
    return lax.dot_general(gg,t,(((1,),(1,)),((),())),preferred_element_type=jnp.float32)
def filt_grad(x, gg):
    C=lax.dot_general(x,gg,(((0,),(0,)),((),())),preferred_element_type=jnp.float32)
    L=C.shape[1]
    z=jnp.zeros((H,H),jnp.float32)
    top=C[:H]; bot=jnp.concatenate([C[H:,H:],z],axis=1)
    D=top+bot
    n=H
    D=jnp.concatenate([D,z],axis=1)
    W=L+H
    lane=None
    while n>1:
        n//=2
        D=D[:n]+pltpu.roll(D[n:],W-n,1)
    return D[:,:L]


VM = pl.BlockSpec(memory_space=pltpu.VMEM)
ANY = pl.BlockSpec(memory_space=pl.ANY)
NC = 8
RA = 384
CH = 128
NA = RA // CH


def kernel(
    q_hbm, k_hbm, v_hbm, t_hbm, w_hbm, og_hbm,
    proj_out, gq_out, gk_out, gv_out, gf_out,
    w, og, tb, xp, gp, sx, sg, yb_, ub_, yr, ur, st, rt, sf, rf,
    sp, r0, ra, rb, acc, dg, cv, go, q_ref, k_ref, v_ref, t_ref,
    proj_ref, gq_ref, gk_ref, gv_ref, gf_ref,
    lsem, osem, ags, agr, sibs, sibr, sps, spr, ras, rar, rbs, rbr, a2s, a2r,
):
    mc = lax.axis_index("ctx")
    mt = lax.axis_index("tp")
    zh, x = mc // 4, mc % 4
    zl, y, co = mt // 8, (mt // 2) % 4, mt % 2
    yd = 1 - 2 * co
    yf, yb, yo = (y + yd + 4) % 4, (y - yd + 4) % 4, (y + 2) % 4
    zp = 1 - zl
    T = lambda z, yy: z * 8 + yy * 2 + co
    M = lambda z, yy: z * 4 + yy
    front, back = (mc, T(zl, yf)), (mc, T(zl, yb))
    zpar, sib = (mc, T(zp, y)), (mc, zl * 8 + y * 2 + 1 - co)
    peers = []
    for k in range(1, NC):
        pc = ((zh + k // 4) % 2) * 4 + (x + k % 4) % 4
        peers.append((k, pc, (pc, mt)))
    G = 4
    L = 512
    RB = L - RA
    scale = 1.0 / math.sqrt(NC * L)

    barrier = pltpu.get_barrier_semaphore()
    partners = [front, back, zpar, sib] + [p[2] for p in peers]
    for d in partners:
        pl.semaphore_signal(barrier, inc=1, device_id=d, device_id_type=MESH)

    def lc(src, dst, sem):
        c = pltpu.make_async_copy(src, dst, sem)
        c.start()
        return c

    kcopy = lc(k_hbm, k_ref, lsem.at[1])
    vcopy = lc(v_hbm, v_ref, lsem.at[2])
    tcopy = lc(t_hbm, t_ref, lsem.at[0])
    qcopy = lc(q_hbm, q_ref, lsem.at[3])
    ocopy = lc(og_hbm, og.at[mt], lsem.at[4])
    wcopy = lc(w_hbm, w, lsem.at[5])

    def spread(dst, full):
        for r in range(NC):
            for g in range(G):
                for ib in range(2):
                    dst[r, g, 16 * ib : 16 * ib + 16, :] = full[
                        64 * r + 16 * g : 64 * r + 16 * g + 16, B * ib : B * ib + B
                    ]

    def joined(src):
        rows = []
        for r in range(NC):
            for g in range(G):
                rows.append(
                    jnp.concatenate([src[r, g, 0:16, :], src[r, g, 16:32, :]], axis=1)
                )
        return jnp.concatenate(rows, axis=0)

    def rc(src, dst, s, r, dev):
        c = pltpu.make_async_remote_copy(
            src_ref=src, dst_ref=dst, send_sem=s, recv_sem=r, device_id=dev, device_id_type=MESH
        )
        c.start()
        return c

    sent = []

    def ag(i, z, yy, lo, n, dev, src=None, j=0):
        slot = T(z, yy)
        if src is None:
            s = og.at[slot, pl.ds(lo, n), :]
        else:
            s = src.at[pl.ds(lo, n), :]
        c = rc(s, og.at[slot, pl.ds(lo, n), :], ags.at[i, j], agr.at[i, j], dev)
        sent.append(c)
        return c

    def aga(i, z, yy, dev, j, src=None):
        return ag(i, z, yy, CH * j, CH, dev, src, j)

    def agb(i, z, yy, dev, src=None):
        return ag(i, z, yy, RA, RB, dev, src)

    def a2a(base, src, dst):
        out = []
        for k, pc, dev in peers:
            c = rc(src(pc), dst, a2s.at[base, k - 1], a2r.at[base, k - 1], dev)
            sent.append(c)
            out.append(c)
        return out

    def recv(cs):
        for c in cs:
            c.wait_recv()

    at32 = lambda c, off: pl.ds(pl.multiple_of(32 * c + off, 32), 32)
    hf = lambda h: pl.ds(2 * h, 2)

    def sibsend(z, yy, src=None):
        slot = T(z, yy)
        m = M(z, yy)
        c = rc(og.at[slot] if src is None else src, og.at[slot], sibs.at[m], sibr.at[m], sib)
        sent.append(c)
        return c

    def sibwait(z, yy):
        slot = z * 8 + yy * 2 + 1 - co
        m = M(z, yy)
        pltpu.make_async_remote_copy(
            src_ref=og.at[slot], dst_ref=og.at[slot], send_sem=sibs.at[m], recv_sem=sibr.at[m],
            device_id=sib, device_id_type=MESH,
        ).wait_recv()

    pl.semaphore_wait(barrier, len(partners))
    J = range(NA)
    m5 = [aga(4, zl, y, zpar, 0, og_hbm)]
    m1 = agb(0, zl, y, front, og_hbm)
    m2 = agb(1, zl, y, back, og_hbm)
    m3 = [aga(2, zl, y, front, j, og_hbm) for j in J]
    m4 = [aga(3, zl, y, back, j, og_hbm) for j in J]
    tcopy.wait()
    for r in range(NC):
        blk = t_ref[G * r : G * r + G, :] * scale
        st[r, 0:G, :] = blk
        st[r, G:8, :] = blk
    tcs = a2a(0, lambda pc: st.at[pc], rt.at[mc])
    kcopy.wait()
    vcopy.wait()
    spread(sx, (k_ref[...].astype(f32) * v_ref[...].astype(f32)).astype(bf).T)
    xcs = [
        a2a(1 + h, lambda pc, h=h: sx.at[pc, hf(h)], xp.at[hf(h), at32(mc, B), :]) for h in (0, 1)
    ]
    for j in range(1, NA):
        m5.append(aga(4, zl, y, zpar, j, og_hbm))
    sibsend(zl, y, og_hbm)

    xp[:, 0:B, :] = jnp.zeros((G, B, B), bf)
    gp[:, B : 2 * B, :] = jnp.zeros((G, B, B), bf)
    xp[:, at32(mc, B), :] = sx[mc]
    rt[mc] = st[mc]
    acc[...] = jnp.zeros(acc.shape, f32)

    m5[0].wait_recv()
    m11 = [aga(10, zp, y, front, 0)]
    m12 = [aga(11, zp, y, back, 0)]
    m1.wait_recv()
    m7 = agb(6, zl, yb, front)
    recv(tcs)
    for g in range(G):
        build_tb(tb, g, jnp.concatenate([rt[s, g : g + 1, :] for s in range(NC)], axis=1))

    def fwd(g, _):
        yb_[g] = conv_fwd(xp, tb, g).astype(bf)
        return 0

    ycs = []
    m3[0].wait_recv()
    m13 = [aga(12, zl, yb, front, 0)]
    for h in (0, 1):
        recv(xcs[h])
        if h == 0:
            m3[1].wait_recv()
            m13.append(aga(12, zl, yb, front, 1))
        lax.fori_loop(2 * h, 2 * h + 2, fwd, 0)
        ycs.append(
            a2a(3 + h, lambda pc, h=h: yb_.at[hf(h), at32(pc, 0), :], yr.at[mc, hf(h)])
        )
        if h == 0:
            for j in range(1, NA):
                m5[j].wait_recv()
                m11.append(aga(10, zp, y, front, j))
                m12.append(aga(11, zp, y, back, j))
            for j in range(2, NA):
                m3[j].wait_recv()
                m13.append(aga(12, zl, yb, front, j))
    yr[mc] = yb_[:, at32(mc, 0), :]
    m6 = agb(5, zl, y, zpar, og_hbm)
    m8 = agb(7, zl, yb, zpar)
    m2.wait_recv()
    m9 = agb(8, zl, yf, zpar)

    sibsend(zl, yb)
    recv(m4)
    sibsend(zl, yf)

    wcopy.wait()
    ocopy.wait()
    qcopy.wait()

    def dstep(z, yy):
        sibwait(z, yy)
        m = M(z, yy)

        def half(h, _):
            rows = pl.ds(pl.multiple_of(h * B, B), B)
            nt = (((1,), (1,)), ((), ()))
            a = lax.dot_general(
                og[2 * m, rows, :], w[:, pl.ds(pl.multiple_of(m * 1024, 1024), 512)],
                nt, preferred_element_type=f32,
            )
            b = lax.dot_general(
                og[2 * m + 1, rows, :], w[:, pl.ds(pl.multiple_of(m * 1024 + 512, 512), 512)],
                nt, preferred_element_type=f32,
            )
            acc[rows, :] += a + b
            return 0

        lax.fori_loop(0, 2, half, 0)

    dstep(zl, y)
    m7.wait_recv()
    m10 = agb(9, zl, yo, zpar)
    m14 = [None] * NA
    for j in range(NA - 1):
        m11[j].wait_recv()
        m14[j] = aga(13, zp, yb, front, j)
    dstep(zl, yb)
    dstep(zl, yf)

    recv(ycs[0])
    recv(ycs[1])
    conv = joined(yr).T
    cv[...] = conv
    go[...] = (q_ref[...].astype(f32) * conv.astype(f32)).astype(bf)

    def psib(o, _):
        z = (zp + o % 2) % 2
        yy = (y + 2 + o // 2) % 4
        m = M(z, yy)
        cols = pl.ds(pl.multiple_of((2 * m + 1 - co) * 512, 512), 512)
        sp[m] = jnp.dot(go[...], w[:, cols], preferred_element_type=f32).astype(bf)
        rc(sp.at[m], r0.at[m], sps.at[m], spr.at[m], sib)
        return 0

    lax.fori_loop(0, 4, psib, 0)
    m11[NA - 1].wait_recv()
    m14[NA - 1] = aga(13, zp, yb, front, NA - 1)
    m6.wait_recv()
    sibsend(zp, y)
    lax.fori_loop(4, 8, psib, 0)

    def spdesc(m):
        return pltpu.make_async_remote_copy(
            src_ref=sp.at[m], dst_ref=r0.at[m], send_sem=sps.at[m], recv_sem=spr.at[m],
            device_id=sib, device_id_type=MESH,
        )

    def own(yy):
        def one(o, _):
            m = M((zp + o) % 2, yy)
            cols = pl.ds(pl.multiple_of((2 * m + co) * 512, 512), 512)
            spdesc(m).wait_recv()
            r0[m] = (
                jnp.dot(go[...], w[:, cols], preferred_element_type=f32) + r0[m].astype(f32)
            ).astype(bf)
            return 0

        lax.fori_loop(0, 2, one, 0)

    def sa(i, j, z, yy, dev):
        c = rc(r0.at[M(z, yy), pl.ds(CH * j, CH), :], ra.at[i, j], ras.at[i, j], rar.at[i, j], dev)
        sent.append(c)
        return c

    def sb(i, z, yy, dev):
        c = rc(r0.at[M(z, yy), pl.ds(RA, RB), :], rb.at[i], rbs.at[i], rbr.at[i], dev)
        sent.append(c)
        return c

    def add(z, yy, lo, n, *parts):
        rows = pl.ds(lo, n)
        m = M(z, yy)
        total = r0[m, rows, :].astype(f32)
        for p in parts:
            total = total + p.astype(f32)
        return total

    def put(z, yy, lo, n, *parts):
        r0[M(z, yy), pl.ds(lo, n), :] = add(z, yy, lo, n, *parts).astype(bf)

    own(yo)
    a2 = [sa(1, j, zp, yo, front) for j in J]
    b1 = sb(0, zp, yo, zpar)
    m8.wait_recv()
    sibsend(zp, yb)
    m9.wait_recv()
    recv(m12)
    sibsend(zp, yf)
    own(yb)
    a4 = [sa(3, j, zp, yb, back) for j in J]
    a1 = [sa(0, j, zl, yo, front) for j in J]
    b2 = sb(1, zp, yb, zpar)
    recv(m13)
    sibsend(zl, yo)
    dstep(zp, y)
    dstep(zp, yb)
    dstep(zp, yf)
    own(yf)
    b3 = sb(2, zp, yf, zpar)
    dstep(zl, yo)
    recv(m14)
    m10.wait_recv()
    sibsend(zp, yo)
    own(y)
    b4 = sb(3, zp, y, zpar)
    dstep(zp, yo)
    dgv = acc[...].astype(bf)
    dg[...] = dgv
    spread(sg, (dgv.astype(f32) * q_ref[...].astype(f32)).astype(bf).T)
    gcs = [
        a2a(5 + h, lambda pc, h=h: sg.at[pc, hf(h)], gp.at[hf(h), at32(mc, 0), :]) for h in (0, 1)
    ]
    gp[:, at32(mc, 0), :] = sg[mc]
    gq_ref[...] = (dg[...].astype(f32) * cv[...].astype(f32)).astype(bf)
    outs = [lc(gq_ref, gq_out, osem.at[0])]

    a5, a6, a7 = [], [], []
    for j in J:
        a2[j].wait_recv()
        put(zp, yf, CH * j, CH, ra[1, j])
        a6.append(sa(5, j, zp, yf, front))
    b1.wait_recv()
    put(zl, yo, RA, RB, rb[0])
    b5 = sb(4, zl, yo, front)
    b2.wait_recv()
    put(zl, yb, RA, RB, rb[1])
    b6 = sb(5, zl, yb, back)
    a3 = [sa(2, j, zl, yb, back) for j in J]
    for j in J:
        a1[j].wait_recv()
        put(zl, yf, CH * j, CH, ra[0, j])
        a5.append(sa(4, j, zl, yf, front))

    def bwd(g, _):
        ub_[g] = conv_bwd(gg_of(gp, g), tmat(tb, g)).astype(bf)
        return 0

    def fgrad(g):
        row = filt_grad(xp[g, B : 2 * B, :], gg_of(gp, g)) * scale
        for r in range(NC):
            sf[r, g : g + 1, :] = row[:, L * r : L * r + L]
            sf[r, G + g : G + g + 1, :] = row[:, L * r : L * r + L]

    ucs = []
    for h in (0, 1):
        recv(gcs[h])
        lax.fori_loop(2 * h, 2 * h + 2, bwd, 0)
        ucs.append(
            a2a(7 + h, lambda pc, h=h: ub_.at[hf(h), at32(pc, 0), :], ur.at[mc, hf(h)])
        )
        if h == 0:
            for j in J:
                a4[j].wait_recv()
                a6[j].wait_recv()
                put(zp, y, CH * j, CH, ra[3, j], ra[5, j])
                a7.append(sa(6, j, zp, y, zpar))
    ur[mc] = ub_[:, at32(mc, 0), :]
    b3.wait_recv()
    b5.wait_recv()
    put(zl, yf, RA, RB, rb[2], rb[4])
    b7 = sb(6, zl, yf, front)
    fgrad(0)
    fgrad(1)
    fgrad(2)
    fgrad(3)
    fcs = a2a(9, lambda pc: sf.at[pc], rf.at[mc])
    rf[mc] = sf[mc]

    recv(ucs[0])
    recv(ucs[1])
    u = joined(ur).T.astype(f32)
    gk_ref[...] = (u * v_ref[...].astype(f32)).astype(bf)
    outs.append(lc(gk_ref, gk_out, osem.at[1]))
    gv_ref[...] = (u * k_ref[...].astype(f32)).astype(bf)
    outs.append(lc(gv_ref, gv_out, osem.at[2]))
    recv(fcs)
    for s in range(NC):
        gf_ref[G * s : G * s + G, :] = rf[s, 0:G, :]
    outs.append(lc(gf_ref, gf_out, osem.at[3]))

    for j in J:
        a3[j].wait_recv()
        a7[j].wait_recv()
        a5[j].wait_recv()
        proj_ref[pl.ds(CH * j, CH), :] = add(
            zl, y, CH * j, CH, ra[2, j], ra[4, j], ra[6, j]
        ).astype(bf)
    b4.wait_recv()
    b6.wait_recv()
    b7.wait_recv()
    proj_ref[pl.ds(RA, RB), :] = add(zl, y, RA, RB, rb[3], rb[5], rb[6]).astype(bf)
    outs.append(lc(proj_ref, proj_out, osem.at[4]))

    for c in sent:
        c.wait_send()

    def drain(m, _):
        spdesc(m).wait_send()
        return 0

    lax.fori_loop(0, 8, drain, 0)
    for c in outs:
        c.wait()


def handover(*refs):
    n = 5
    ins, outs, held, sem = refs[:n], refs[n : 2 * n], refs[2 * n : 3 * n], refs[-1]
    first = [pltpu.make_async_copy(ins[i], held[i], sem.at[0, i]) for i in range(n)]
    then = [pltpu.make_async_copy(held[i], outs[i], sem.at[1, i]) for i in range(n)]
    for c in first:
        c.start()
    for i in range(n):
        first[i].wait()
        then[i].start()
    for c in then:
        c.wait()


def local(query_gate, key_gate, value_input, filter_taps, out_weight, out_grad):
    L, D = query_gate.shape
    G = 4
    blk = jax.ShapeDtypeStruct((L, D), bf)
    vm = pltpu.VMEM
    dma = pltpu.SemaphoreType.DMA
    shapes = (blk, blk, blk, blk, jax.ShapeDtypeStruct(filter_taps.shape[::-1], f32))
    parts = pl.pallas_call(
        kernel,
        in_specs=[ANY] * 6,
        out_specs=(ANY,) * 5,
        out_shape=shapes,
        scratch_shapes=[
            vm(out_weight.shape, bf),
            vm((16, L, D), bf),
            vm((G, H, NC * L + 2 * H), bf),
            vm((G, 2 * B, B), bf),
            vm((G, 2 * B, B), bf),
            vm((NC, G, 32, B), bf),
            vm((NC, G, 32, B), bf),
            vm((G, B, B), bf),
            vm((G, B, B), bf),
            vm((NC, G, 32, B), bf),
            vm((NC, G, 32, B), bf),
            vm((NC, 8, L), f32),
            vm((NC, 8, L), f32),
            vm((NC, 8, L), f32),
            vm((NC, 8, L), f32),
            vm((8, L, D), bf),
            vm((8, L, D), bf),
            vm((7, NA, CH, D), bf),
            vm((7, L - RA, D), bf),
            vm((L, D), f32),
            vm((L, D), bf),
            vm((L, D), bf),
            vm((L, D), bf),
            vm((L, D), bf),
            vm((L, D), bf),
            vm((L, D), bf),
            vm((filter_taps.shape[1], L), f32),
            vm((L, D), bf),
            vm((L, D), bf),
            vm((L, D), bf),
            vm((L, D), bf),
            vm((filter_taps.shape[1], L), f32),
            dma((6,)), dma((5,)),
            dma((14, NA)), dma((14, NA)),
            dma((8,)), dma((8,)),
            dma((8,)), dma((8,)),
            dma((7, NA)), dma((7, NA)),
            dma((7,)), dma((7,)),
            dma((10, NC - 1)), dma((10, NC - 1)),
        ],
        compiler_params=pltpu.CompilerParams(
            collective_id=0, has_side_effects=True, vmem_limit_bytes=62 << 20
        ),
        name="hyena",
    )(query_gate, key_gate, value_input, filter_taps.T, out_weight, out_grad)
    done = pl.pallas_call(
        handover,
        in_specs=[ANY] * 5,
        out_specs=(ANY,) * 5,
        out_shape=shapes,
        scratch_shapes=[vm(a.shape, a.dtype) for a in shapes] + [dma((2, 5))],
        name="handover",
    )(*parts)
    return (*done[:4], done[4].T)


def solution(mesh):
    spec = P("ctx", "tp")
    return jax.shard_map(
        local,
        mesh=mesh,
        in_specs=(spec, spec, spec, spec, P("tp", None), spec),
        out_specs=(spec,) * 5,
        check_vma=False,
    )
```

```python
import math

import jax
import jax.numpy as jnp
from jax import lax
from jax.experimental import pallas as pl
from jax.experimental.pallas import tpu as pltpu
from jax.sharding import PartitionSpec as P

MESH = pl.DeviceIdType.MESH
f32 = jnp.float32
bf = jnp.bfloat16
B=256; H=128
def build_tb(tb_ref, g, taps_row):
    L=taps_row.shape[1]
    z=jnp.zeros((1,H),jnp.float32)
    v=jnp.broadcast_to(jnp.concatenate([z,taps_row,z],axis=1),(16,L+2*H))
    base=pltpu.roll(v,0,1,stride=1,stride_axis=0)
    for k in range(H//16):
        r=pltpu.roll(base,16*k,1) if k else base
        tb_ref[g,16*k:16*k+16,:]=r.astype(jnp.bfloat16)
def tmat(tb_ref,g):
    L=tb_ref.shape[2]-2*H
    return jnp.concatenate([tb_ref[g,:,H:H+L],tb_ref[g,:,0:L]],axis=0)
def conv_fwd(xp_ref, tb_ref, g):
    R=xp_ref.shape[1]//2; nb=R//16
    acc=None
    xs=[xp_ref[g,R-16*d:2*R-16*d,:] for d in range(nb)]
    ts=[jnp.concatenate([tb_ref[g,:,H+B*d:H+B*d+B],tb_ref[g,:,B*d:B*d+B]],axis=0) for d in range(nb)]
    return jnp.dot(jnp.concatenate(xs,axis=1),jnp.concatenate(ts,axis=0),preferred_element_type=jnp.float32)
def gg_of(gp_ref,g):
    R=gp_ref.shape[1]//2; nb=R//16
    return jnp.concatenate([gp_ref[g,16*d:16*d+R,:] for d in range(nb)],axis=1)
def conv_bwd(gg, t):
    return lax.dot_general(gg,t,(((1,),(1,)),((),())),preferred_element_type=jnp.float32)
def filt_grad(x, gg):
    C=lax.dot_general(x,gg,(((0,),(0,)),((),())),preferred_element_type=jnp.float32)
    L=C.shape[1]
    z=jnp.zeros((H,H),jnp.float32)
    top=C[:H]; bot=jnp.concatenate([C[H:,H:],z],axis=1)
    D=top+bot
    n=H
    D=jnp.concatenate([D,z],axis=1)
    W=L+H
    lane=None
    while n>1:
        n//=2
        D=D[:n]+pltpu.roll(D[n:],W-n,1)
    return D[:,:L]


VM = pl.BlockSpec(memory_space=pltpu.VMEM)
ANY = pl.BlockSpec(memory_space=pl.ANY)
NC = 8
RA = 384
CH = 128
NA = RA // CH
SA = 400
SC = 80
NS = SA // SC


def kernel(
    q_hbm, k_hbm, v_hbm, t_hbm, w_hbm, og_hbm,
    proj_out, gq_out, gk_out, gv_out, gf_out,
    w, og, tb, xp, gp, sx, sg, yb_, ub_, yr, ur, st, rt, sf, rf,
    sp, r0, ra, rb, acc, dg, cv, go, q_ref, k_ref, v_ref, t_ref,
    proj_ref, gq_ref, gk_ref, gv_ref, gf_ref,
    lsem, osem, ags, agr, sibs, sibr, sps, spr, ras, rar, rbs, rbr, a2s, a2r,
):
    mc = lax.axis_index("ctx")
    mt = lax.axis_index("tp")
    zh, x = mc // 4, mc % 4
    zl, y, co = mt // 8, (mt // 2) % 4, mt % 2
    yd = 1 - 2 * co
    yf, yb, yo = (y + yd + 4) % 4, (y - yd + 4) % 4, (y + 2) % 4
    zp = 1 - zl
    T = lambda z, yy: z * 8 + yy * 2 + co
    M = lambda z, yy: z * 4 + yy
    front, back = (mc, T(zl, yf)), (mc, T(zl, yb))
    zpar, sib = (mc, T(zp, y)), (mc, zl * 8 + y * 2 + 1 - co)
    peers = []
    for k in range(1, NC):
        pc = ((zh + k // 4) % 2) * 4 + (x + k % 4) % 4
        peers.append((k, pc, (pc, mt)))
    G = 4
    L = 512
    RB = L - RA
    scale = 1.0 / math.sqrt(NC * L)

    barrier = pltpu.get_barrier_semaphore()
    partners = [front, back, zpar, sib] + [p[2] for p in peers]
    for d in partners:
        pl.semaphore_signal(barrier, inc=1, device_id=d, device_id_type=MESH)

    def lc(src, dst, sem):
        c = pltpu.make_async_copy(src, dst, sem)
        c.start()
        return c

    kcopy = lc(k_hbm, k_ref, lsem.at[1])
    vcopy = lc(v_hbm, v_ref, lsem.at[2])
    tcopy = lc(t_hbm, t_ref, lsem.at[0])
    qcopy = lc(q_hbm, q_ref, lsem.at[3])
    ocopy = lc(og_hbm, og.at[mt], lsem.at[4])
    wcopy = lc(w_hbm, w, lsem.at[5])

    def spread(dst, full):
        for r in range(NC):
            for g in range(G):
                for ib in range(2):
                    dst[r, g, 16 * ib : 16 * ib + 16, :] = full[
                        64 * r + 16 * g : 64 * r + 16 * g + 16, B * ib : B * ib + B
                    ]

    def joined(src):
        rows = []
        for r in range(NC):
            for g in range(G):
                rows.append(
                    jnp.concatenate([src[r, g, 0:16, :], src[r, g, 16:32, :]], axis=1)
                )
        return jnp.concatenate(rows, axis=0)

    def rc(src, dst, s, r, dev):
        c = pltpu.make_async_remote_copy(
            src_ref=src, dst_ref=dst, send_sem=s, recv_sem=r, device_id=dev, device_id_type=MESH
        )
        c.start()
        return c

    sent = []

    def ag(i, z, yy, lo, n, dev, src=None, j=0):
        slot = T(z, yy)
        if src is None:
            s = og.at[slot, pl.ds(lo, n), :]
        else:
            s = src.at[pl.ds(lo, n), :]
        c = rc(s, og.at[slot, pl.ds(lo, n), :], ags.at[i, j], agr.at[i, j], dev)
        sent.append(c)
        return c

    def aga(i, z, yy, dev, j, src=None):
        return ag(i, z, yy, CH * j, CH, dev, src, j)

    def agb(i, z, yy, dev, src=None):
        return ag(i, z, yy, RA, RB, dev, src)

    def a2a(base, src, dst):
        out = []
        for k, pc, dev in peers:
            c = rc(src(pc), dst, a2s.at[base, k - 1], a2r.at[base, k - 1], dev)
            sent.append(c)
            out.append(c)
        return out

    def recv(cs):
        for c in cs:
            c.wait_recv()

    at32 = lambda c, off: pl.ds(pl.multiple_of(32 * c + off, 32), 32)
    hf = lambda h: pl.ds(2 * h, 2)

    def sibsend(z, yy, src=None):
        slot = T(z, yy)
        m = M(z, yy)
        c = rc(og.at[slot] if src is None else src, og.at[slot], sibs.at[m], sibr.at[m], sib)
        sent.append(c)
        return c

    def sibwait(z, yy):
        slot = z * 8 + yy * 2 + 1 - co
        m = M(z, yy)
        pltpu.make_async_remote_copy(
            src_ref=og.at[slot], dst_ref=og.at[slot], send_sem=sibs.at[m], recv_sem=sibr.at[m],
            device_id=sib, device_id_type=MESH,
        ).wait_recv()

    pl.semaphore_wait(barrier, len(partners))
    J = range(NA)
    m5 = [aga(4, zl, y, zpar, 0, og_hbm)]
    m1 = agb(0, zl, y, front, og_hbm)
    m2 = agb(1, zl, y, back, og_hbm)
    m3 = [aga(2, zl, y, front, j, og_hbm) for j in J]
    m4 = [aga(3, zl, y, back, j, og_hbm) for j in J]
    tcopy.wait()
    for r in range(NC):
        blk = t_ref[G * r : G * r + G, :] * scale
        st[r, 0:G, :] = blk
        st[r, G:8, :] = blk
    tcs = a2a(0, lambda pc: st.at[pc], rt.at[mc])
    kcopy.wait()
    vcopy.wait()
    spread(sx, (k_ref[...].astype(f32) * v_ref[...].astype(f32)).astype(bf).T)
    xcs = [
        a2a(1 + h, lambda pc, h=h: sx.at[pc, hf(h)], xp.at[hf(h), at32(mc, B), :]) for h in (0, 1)
    ]
    for j in range(1, NA):
        m5.append(aga(4, zl, y, zpar, j, og_hbm))
    sibsend(zl, y, og_hbm)

    xp[:, 0:B, :] = jnp.zeros((G, B, B), bf)
    gp[:, B : 2 * B, :] = jnp.zeros((G, B, B), bf)
    xp[:, at32(mc, B), :] = sx[mc]
    rt[mc] = st[mc]
    acc[...] = jnp.zeros(acc.shape, f32)

    m5[0].wait_recv()
    m11 = [aga(10, zp, y, front, 0)]
    m12 = [aga(11, zp, y, back, 0)]
    m1.wait_recv()
    m7 = agb(6, zl, yb, front)
    recv(tcs)
    for g in range(G):
        build_tb(tb, g, jnp.concatenate([rt[s, g : g + 1, :] for s in range(NC)], axis=1))

    def fwd(g, _):
        yb_[g] = conv_fwd(xp, tb, g).astype(bf)
        return 0

    ycs = []
    m3[0].wait_recv()
    m13 = [aga(12, zl, yb, front, 0)]
    for h in (0, 1):
        recv(xcs[h])
        if h == 0:
            m3[1].wait_recv()
            m13.append(aga(12, zl, yb, front, 1))
        lax.fori_loop(2 * h, 2 * h + 2, fwd, 0)
        ycs.append(
            a2a(3 + h, lambda pc, h=h: yb_.at[hf(h), at32(pc, 0), :], yr.at[mc, hf(h)])
        )
        if h == 0:
            for j in range(1, NA):
                m5[j].wait_recv()
                m11.append(aga(10, zp, y, front, j))
                m12.append(aga(11, zp, y, back, j))
            for j in range(2, NA):
                m3[j].wait_recv()
                m13.append(aga(12, zl, yb, front, j))
    yr[mc] = yb_[:, at32(mc, 0), :]
    m6 = agb(5, zl, y, zpar, og_hbm)
    m8 = agb(7, zl, yb, zpar)
    m2.wait_recv()
    m9 = agb(8, zl, yf, zpar)

    sibsend(zl, yb)
    recv(m4)
    sibsend(zl, yf)

    wcopy.wait()
    ocopy.wait()
    qcopy.wait()

    def dstep(z, yy):
        sibwait(z, yy)
        m = M(z, yy)

        def half(h, _):
            rows = pl.ds(pl.multiple_of(h * B, B), B)
            nt = (((1,), (1,)), ((), ()))
            a = lax.dot_general(
                og[2 * m, rows, :], w[:, pl.ds(pl.multiple_of(m * 1024, 1024), 512)],
                nt, preferred_element_type=f32,
            )
            b = lax.dot_general(
                og[2 * m + 1, rows, :], w[:, pl.ds(pl.multiple_of(m * 1024 + 512, 512), 512)],
                nt, preferred_element_type=f32,
            )
            acc[rows, :] += a + b
            return 0

        lax.fori_loop(0, 2, half, 0)

    dstep(zl, y)
    m7.wait_recv()
    m10 = agb(9, zl, yo, zpar)
    m14 = [None] * NA
    for j in range(NA - 1):
        m11[j].wait_recv()
        m14[j] = aga(13, zp, yb, front, j)
    dstep(zl, yb)
    dstep(zl, yf)

    recv(ycs[0])
    recv(ycs[1])
    conv = joined(yr).T
    cv[...] = conv
    go[...] = (q_ref[...].astype(f32) * conv.astype(f32)).astype(bf)

    def psib(o, _):
        z = (zp + o % 2) % 2
        yy = (y + 2 + o // 2) % 4
        m = M(z, yy)
        cols = pl.ds(pl.multiple_of((2 * m + 1 - co) * 512, 512), 512)
        sp[m] = jnp.dot(go[...], w[:, cols], preferred_element_type=f32).astype(bf)
        rc(sp.at[m], r0.at[m], sps.at[m], spr.at[m], sib)
        return 0

    lax.fori_loop(0, 4, psib, 0)
    m11[NA - 1].wait_recv()
    m14[NA - 1] = aga(13, zp, yb, front, NA - 1)
    m6.wait_recv()
    sibsend(zp, y)
    lax.fori_loop(4, 8, psib, 0)

    def spdesc(m):
        return pltpu.make_async_remote_copy(
            src_ref=sp.at[m], dst_ref=r0.at[m], send_sem=sps.at[m], recv_sem=spr.at[m],
            device_id=sib, device_id_type=MESH,
        )

    def own(yy):
        def one(o, _):
            m = M((zp + o) % 2, yy)
            cols = pl.ds(pl.multiple_of((2 * m + co) * 512, 512), 512)
            spdesc(m).wait_recv()
            r0[m] = (
                jnp.dot(go[...], w[:, cols], preferred_element_type=f32) + r0[m].astype(f32)
            ).astype(bf)
            return 0

        lax.fori_loop(0, 2, one, 0)

    JR = range(NS)
    SB = L - SA

    def sa(i, j, z, yy, dev):
        c = rc(r0.at[M(z, yy), pl.ds(SC * j, SC), :], ra.at[i, j], ras.at[i, j], rar.at[i, j], dev)
        sent.append(c)
        return c

    def sb(i, z, yy, dev):
        c = rc(r0.at[M(z, yy), pl.ds(SA, SB), :], rb.at[i], rbs.at[i], rbr.at[i], dev)
        sent.append(c)
        return c

    def add(z, yy, lo, n, *parts):
        rows = pl.ds(lo, n)
        m = M(z, yy)
        total = r0[m, rows, :].astype(f32)
        for p in parts:
            total = total + p.astype(f32)
        return total

    def put(z, yy, lo, n, *parts):
        r0[M(z, yy), pl.ds(lo, n), :] = add(z, yy, lo, n, *parts).astype(bf)

    own(yo)
    a2 = [sa(1, j, zp, yo, front) for j in JR]
    b1 = sb(0, zp, yo, zpar)
    m8.wait_recv()
    sibsend(zp, yb)
    m9.wait_recv()
    recv(m12)
    sibsend(zp, yf)
    own(yb)
    a4 = [sa(3, j, zp, yb, back) for j in JR]
    a1 = [sa(0, j, zl, yo, front) for j in JR]
    b2 = sb(1, zp, yb, zpar)
    recv(m13)
    sibsend(zl, yo)
    dstep(zp, y)
    dstep(zp, yb)
    dstep(zp, yf)
    own(yf)
    b3 = sb(2, zp, yf, zpar)
    dstep(zl, yo)
    recv(m14)
    m10.wait_recv()
    sibsend(zp, yo)
    own(y)
    b4 = sb(3, zp, y, zpar)
    dstep(zp, yo)
    dgv = acc[...].astype(bf)
    dg[...] = dgv
    spread(sg, (dgv.astype(f32) * q_ref[...].astype(f32)).astype(bf).T)
    gcs = [
        a2a(5 + h, lambda pc, h=h: sg.at[pc, hf(h)], gp.at[hf(h), at32(mc, 0), :]) for h in (0, 1)
    ]
    gp[:, at32(mc, 0), :] = sg[mc]
    gq_ref[...] = (dg[...].astype(f32) * cv[...].astype(f32)).astype(bf)
    outs = [lc(gq_ref, gq_out, osem.at[0])]

    a5, a6, a7 = [], [], []
    for j in JR:
        a2[j].wait_recv()
        put(zp, yf, SC * j, SC, ra[1, j])
        a6.append(sa(5, j, zp, yf, front))
    b1.wait_recv()
    put(zl, yo, SA, SB, rb[0])
    b5 = sb(4, zl, yo, front)
    b2.wait_recv()
    put(zl, yb, SA, SB, rb[1])
    b6 = sb(5, zl, yb, back)
    a3 = [sa(2, j, zl, yb, back) for j in JR]
    for j in JR:
        a1[j].wait_recv()
        put(zl, yf, SC * j, SC, ra[0, j])
        a5.append(sa(4, j, zl, yf, front))

    def bwd(g, _):
        ub_[g] = conv_bwd(gg_of(gp, g), tmat(tb, g)).astype(bf)
        return 0

    def fgrad(g):
        row = filt_grad(xp[g, B : 2 * B, :], gg_of(gp, g)) * scale
        for r in range(NC):
            sf[r, g : g + 1, :] = row[:, L * r : L * r + L]
            sf[r, G + g : G + g + 1, :] = row[:, L * r : L * r + L]

    ucs = []
    for h in (0, 1):
        recv(gcs[h])
        lax.fori_loop(2 * h, 2 * h + 2, bwd, 0)
        ucs.append(
            a2a(7 + h, lambda pc, h=h: ub_.at[hf(h), at32(pc, 0), :], ur.at[mc, hf(h)])
        )
        if h == 0:
            for j in JR:
                a4[j].wait_recv()
                a6[j].wait_recv()
                put(zp, y, SC * j, SC, ra[3, j], ra[5, j])
                a7.append(sa(6, j, zp, y, zpar))
    ur[mc] = ub_[:, at32(mc, 0), :]
    b3.wait_recv()
    b5.wait_recv()
    put(zl, yf, SA, SB, rb[2], rb[4])
    b7 = sb(6, zl, yf, front)
    fgrad(0)
    fgrad(1)
    fgrad(2)
    fgrad(3)
    fcs = a2a(9, lambda pc: sf.at[pc], rf.at[mc])
    rf[mc] = sf[mc]

    recv(ucs[0])
    recv(ucs[1])
    u = joined(ur).T.astype(f32)
    gk_ref[...] = (u * v_ref[...].astype(f32)).astype(bf)
    outs.append(lc(gk_ref, gk_out, osem.at[1]))
    gv_ref[...] = (u * k_ref[...].astype(f32)).astype(bf)
    outs.append(lc(gv_ref, gv_out, osem.at[2]))
    recv(fcs)
    for s in range(NC):
        gf_ref[G * s : G * s + G, :] = rf[s, 0:G, :]
    outs.append(lc(gf_ref, gf_out, osem.at[3]))

    for j in JR:
        a3[j].wait_recv()
        a7[j].wait_recv()
        a5[j].wait_recv()
        proj_ref[pl.ds(SC * j, SC), :] = add(
            zl, y, SC * j, SC, ra[2, j], ra[4, j], ra[6, j]
        ).astype(bf)
    b4.wait_recv()
    b6.wait_recv()
    b7.wait_recv()
    proj_ref[pl.ds(SA, SB), :] = add(zl, y, SA, SB, rb[3], rb[5], rb[6]).astype(bf)
    outs.append(lc(proj_ref, proj_out, osem.at[4]))

    for c in sent:
        c.wait_send()

    def drain(m, _):
        spdesc(m).wait_send()
        return 0

    lax.fori_loop(0, 8, drain, 0)
    for c in outs:
        c.wait()


def handover(*refs):
    n = 5
    ins, outs, held, sem = refs[:n], refs[n : 2 * n], refs[2 * n : 3 * n], refs[-1]
    first = [pltpu.make_async_copy(ins[i], held[i], sem.at[0, i]) for i in range(n)]
    then = [pltpu.make_async_copy(held[i], outs[i], sem.at[1, i]) for i in range(n)]
    for c in first:
        c.start()
    for i in range(n):
        first[i].wait()
        then[i].start()
    for c in then:
        c.wait()


def local(query_gate, key_gate, value_input, filter_taps, out_weight, out_grad):
    L, D = query_gate.shape
    G = 4
    blk = jax.ShapeDtypeStruct((L, D), bf)
    vm = pltpu.VMEM
    dma = pltpu.SemaphoreType.DMA
    shapes = (blk, blk, blk, blk, jax.ShapeDtypeStruct(filter_taps.shape[::-1], f32))
    parts = pl.pallas_call(
        kernel,
        in_specs=[ANY] * 6,
        out_specs=(ANY,) * 5,
        out_shape=shapes,
        scratch_shapes=[
            vm(out_weight.shape, bf),
            vm((16, L, D), bf),
            vm((G, H, NC * L + 2 * H), bf),
            vm((G, 2 * B, B), bf),
            vm((G, 2 * B, B), bf),
            vm((NC, G, 32, B), bf),
            vm((NC, G, 32, B), bf),
            vm((G, B, B), bf),
            vm((G, B, B), bf),
            vm((NC, G, 32, B), bf),
            vm((NC, G, 32, B), bf),
            vm((NC, 8, L), f32),
            vm((NC, 8, L), f32),
            vm((NC, 8, L), f32),
            vm((NC, 8, L), f32),
            vm((8, L, D), bf),
            vm((8, L, D), bf),
            vm((7, NS, SC, D), bf),
            vm((7, L - SA, D), bf),
            vm((L, D), f32),
            vm((L, D), bf),
            vm((L, D), bf),
            vm((L, D), bf),
            vm((L, D), bf),
            vm((L, D), bf),
            vm((L, D), bf),
            vm((filter_taps.shape[1], L), f32),
            vm((L, D), bf),
            vm((L, D), bf),
            vm((L, D), bf),
            vm((L, D), bf),
            vm((filter_taps.shape[1], L), f32),
            dma((6,)), dma((5,)),
            dma((14, NA)), dma((14, NA)),
            dma((8,)), dma((8,)),
            dma((8,)), dma((8,)),
            dma((7, NS)), dma((7, NS)),
            dma((7,)), dma((7,)),
            dma((10, NC - 1)), dma((10, NC - 1)),
        ],
        compiler_params=pltpu.CompilerParams(
            collective_id=0, has_side_effects=True, vmem_limit_bytes=62 << 20
        ),
        name="hyena",
    )(query_gate, key_gate, value_input, filter_taps.T, out_weight, out_grad)
    done = pl.pallas_call(
        handover,
        in_specs=[ANY] * 5,
        out_specs=(ANY,) * 5,
        out_shape=shapes,
        scratch_shapes=[vm(a.shape, a.dtype) for a in shapes] + [dma((2, 5))],
        name="handover",
    )(*parts)
    return (*done[:4], done[4].T)


def solution(mesh):
    spec = P("ctx", "tp")
    return jax.shard_map(
        local,
        mesh=mesh,
        in_specs=(spec, spec, spec, spec, P("tp", None), spec),
        out_specs=(spec,) * 5,
        check_vma=False,
    )
```
